32 devices in a mesh: fsdp: 32 (over z, y, x, core).
Axes of the slice: x: 2, y: 2, z: 4, core: 2. Of those that a mesh axis runs over, the one named last changes fastest.
Arguments:
- hidden: bfloat16 [8192, 768], P('fsdp'), may hold values from -6 to 6
- cotangent: bfloat16 [8192, 768], P('fsdp'), may hold values from -6 to 6
- seq_lengths: int32 [64], P('fsdp'), may hold values from 0 to 256, as said below
- w_qkv: bfloat16 [768, 2304], P('fsdp'), may hold values from -0.21875 to 0.21875
- b_qv: bfloat16 [1536], P('fsdp'), may hold values from -4 to 4
- w_out: bfloat16 [768, 768], P('fsdp'), may hold values from -1.25 to 1.25
- b_out: bfloat16 [768], P('fsdp'), may hold values from -3 to 3
- gain_one: bfloat16 [768], P('fsdp'), may hold values from 0.25 to 1.75
- shift_one: bfloat16 [768], P('fsdp'), may hold values from -3 to 3
- w_in: bfloat16 [768, 3072], P('fsdp'), may hold values from -0.21875 to 0.21875
- b_in: bfloat16 [3072], P('fsdp'), may hold values from -3 to 3
- w_back: bfloat16 [3072, 768], P('fsdp'), may hold values from -0.109375 to 0.109375
- b_back: bfloat16 [768], P('fsdp'), may hold values from -3 to 3
- gain_two: bfloat16 [768], P('fsdp'), may hold values from 0.25 to 1.75
- shift_two: bfloat16 [768], P('fsdp'), may hold values from -3 to 3
Outputs:
- output: bfloat16 [8192, 768], P('fsdp')
- grad_hidden: bfloat16 [8192, 768], P('fsdp')
- grad_w_qkv: float32 [768, 2304], P('fsdp')
- grad_b_qv: float32 [1536], P('fsdp')
- grad_w_out: float32 [768, 768], P('fsdp')
- grad_b_out: float32 [768], P('fsdp')
- grad_gain_one: float32 [768], P('fsdp')
- grad_shift_one: float32 [768], P('fsdp')
- grad_w_in: float32 [768, 3072], P('fsdp')
- grad_b_in: float32 [3072], P('fsdp')
- grad_w_back: float32 [3072, 768], P('fsdp')
- grad_b_back: float32 [768], P('fsdp')
- grad_gain_two: float32 [768], P('fsdp')
- grad_shift_two: float32 [768], P('fsdp')
The draws below stay inside these ranges and needn't reach their ends.
Inputs may be any that keep to these rules, and one draw needn't show every extreme that they name: `seq_lengths`: block 0 of every device's 2 blocks begins a sequence; a sequence of length L that begins at block j lies within the device's blocks, and the next nonzero entry comes at block j + ceil(L / 128) or later. Some device holds one sequence of 256 tokens.
All inputs are finite; a program needn't handle non-finite values.
Results may differ from the reference program's by a relative error of at most 0.014.
Values may be sent and summed in bfloat16 or wider, within the bound.
A program may use at most 128 MiB of HBM per device.

```python
import math
import jax
import jax.numpy as jnp
from jax import lax

D = 768
HEAD_DIM = 64
FF = 3072
BLOCK = 128
BLK_DEV = 2
TOK_DEV = 256
SLOTS = 64
TOKENS = 8192
N_FSDP = 32


def draw_seq_lengths(key, part):
    key = jax.random.fold_in(key, 11)
    key_flags = jax.random.fold_in(key, 1)
    key_sizes = jax.random.fold_in(key, 2)
    key_whole = jax.random.fold_in(key, 3)
    device_rows = SLOTS // BLK_DEV
    block_ids = jnp.arange(BLK_DEV, dtype=jnp.int32)
    flags = jax.random.randint(key_flags, (device_rows, BLK_DEV), 0, 2).astype(jnp.int32)
    flags = jnp.where(block_ids[None, :] == 0, 1, flags)
    picked = jax.random.randint(key_whole, (), 0, device_rows)
    whole_row = jnp.arange(device_rows, dtype=jnp.int32)[:, None] == picked
    flags = jnp.where(whole_row & (block_ids[None, :] > 0), 0, flags)
    later = (block_ids[None, None, :] > block_ids[None, :, None]) & (flags[:, None, :] == 1)
    following = jnp.min(jnp.where(later, block_ids[None, None, :], BLK_DEV), axis=2)
    span_blocks = following - block_ids[None, :]
    drawn = jax.random.randint(key_sizes, (device_rows, BLK_DEV), 1, span_blocks * BLOCK + 1).astype(jnp.int32)
    drawn = jnp.where(whole_row & (block_ids[None, :] == 0), BLK_DEV * BLOCK, drawn)
    return (flags * drawn).astype(jnp.int32).reshape(SLOTS)


def level_of(rng, dims, split, smallest, largest):
    level, own = 1.0, jax.random.fold_in(rng, 6)
    for dim, shards_of in split:
        heights = jnp.exp(jax.random.uniform(jax.random.fold_in(own, dim), (shards_of,), jnp.float32, smallest / len(split), largest / len(split)))
        level = level * jnp.repeat(heights, dims[dim] // shards_of).reshape([-1 if axis == dim else 1 for axis in range(len(dims))])
    return level


def scatter_about(own_key, shape, width, most, cuts=(), held_as=jnp.bfloat16):
    values = jax.random.normal(own_key, shape, jnp.float32) * width
    if len(cuts) > 0:
        values = level_of(own_key, shape, cuts, -0.22, 0.18) * values
    return jnp.clip(values, min=-most, max=most).astype(held_as)


def setup_inputs(seed: int = 0) -> dict:
    streams_of = jax.random.split(jax.random.key(seed), 16)
    return {
        "hidden": scatter_about(streams_of[0], (TOKENS, D), 1.0, 6.0, ((0, 32),)),
        "cotangent": scatter_about(streams_of[1], (TOKENS, D), 1.0, 6.0, ((0, 32),)),
        "seq_lengths": draw_seq_lengths(jax.random.fold_in(streams_of[15], 71), 0),
        "w_qkv": scatter_about(streams_of[3], (D, 3 * D), D ** -0.5, 0.21875, ((0, 32),)),
        "b_qv": scatter_about(streams_of[4], (2 * D,), 1.0, 4.0, ((0, 32),)),
        "w_out": scatter_about(streams_of[5], (D, D), (D // 32) ** -0.5, 1.25, ((0, 32),)),
        "b_out": scatter_about(streams_of[6], (D,), 0.5, 3.0, ((0, 32),)),
        "gain_one": jnp.clip(1.0 + 0.15 * jax.random.normal(streams_of[7], (D,), jnp.float32), 0.25, 1.75).astype(jnp.bfloat16),
        "shift_one": scatter_about(streams_of[8], (D,), 0.5, 3.0, ((0, 32),)),
        "w_in": scatter_about(streams_of[9], (D, FF), D ** -0.5, 0.21875, ((0, 32),)),
        "b_in": scatter_about(streams_of[10], (FF,), 0.5, 3.0, ((0, 32),)),
        "w_back": scatter_about(streams_of[11], (FF, D), FF ** -0.5, 0.109375, ((0, 32),)),
        "b_back": scatter_about(streams_of[12], (D,), 0.5, 3.0, ((0, 32),)),
        "gain_two": jnp.clip(1.0 + 0.15 * jax.random.normal(streams_of[13], (D,), jnp.float32), 0.25, 1.75).astype(jnp.bfloat16),
        "shift_two": scatter_about(streams_of[14], (D,), 0.5, 3.0, ((0, 32),)),
    }


@jax.custom_vjp
def low(v):
    return lax.optimization_barrier(v.astype(jnp.bfloat16)).astype(jnp.float32)

@jax.custom_vjp
def low_back(v):
    return v

def low_keep(v):
    return (low(v), None)

def low_pass(kept, grad):
    return (grad,)

def back_keep(v):
    return (v, None)

def back_low(kept, grad):
    return (low(grad),)
low.defvjp(low_keep, low_pass)
low_back.defvjp(back_keep, back_low)
EPSILON = 1e-12
PRECISE = lax.Precision.HIGHEST

def layer_norm(values, gain, shift):
    centre = values - lax.optimization_barrier(jnp.mean(values, axis=-1, keepdims=True))
    spread = lax.optimization_barrier(jnp.mean(centre * centre, axis=-1, keepdims=True))
    return centre * lax.rsqrt(spread + EPSILON) * gain + shift

def smooth_gate(values):
    return jax.nn.gelu(values, approximate=False)

def seq_masks(lengths, row_count):
    blocks = lengths.shape[0]
    block_width = row_count // blocks
    block_ids = jnp.arange(blocks, dtype=jnp.int32)
    starts = jnp.where(lengths > 0, block_ids, 0).astype(jnp.int32)
    owners = lax.cummax(starts, axis=0)
    position = jnp.arange(row_count, dtype=jnp.int32)
    member = position[:, None] // block_width == block_ids[None, :]
    owner_row = lax.optimization_barrier(jnp.sum(jnp.where(member, owners[None, :], 0), axis=1)).astype(jnp.int32)
    chosen = owner_row[:, None] == block_ids[None, :]
    length_row = lax.optimization_barrier(jnp.sum(jnp.where(chosen, lengths[None, :], 0), axis=1)).astype(jnp.int32)
    alive_row = position - owner_row * block_width < length_row
    same_seq = (owner_row[:, None] == owner_row[None, :]) & alive_row[None, :]
    return (alive_row, same_seq)

def matmul(left, right):
    return jnp.dot(left, right, precision=PRECISE)

def buffer_layer(tokens, lengths, weights):
    w_qkv, b_qv, w_out, b_out, gain_one, shift_one, w_in, b_in, w_back, b_back, gain_two, shift_two = weights
    row_count, model_width = tokens.shape
    head_count = model_width // HEAD_DIM
    alive_row, same_seq = seq_masks(lengths, row_count)
    alive_col = alive_row.astype(jnp.float32)[:, None]
    bias_qkv = jnp.concatenate([b_qv[:model_width], jnp.zeros((model_width,), jnp.float32), b_qv[model_width:]])
    qkv_low = low(low_back(matmul(tokens, w_qkv) + bias_qkv))
    queries = qkv_low[:, :model_width].reshape(row_count, head_count, HEAD_DIM)
    keys_all = qkv_low[:, model_width:2 * model_width].reshape(row_count, head_count, HEAD_DIM)
    values_all = qkv_low[:, 2 * model_width:].reshape(row_count, head_count, HEAD_DIM)
    raw_scores = jnp.einsum('qhd,khd->hqk', queries, keys_all, precision=PRECISE) * HEAD_DIM ** (-0.5)
    scores = jnp.where(same_seq[None], low_back(raw_scores), -1e+30)
    probs_low = low(jax.nn.softmax(scores, axis=-1))
    attended = jnp.einsum('hqk,khd->qhd', probs_low, values_all, precision=PRECISE).reshape(row_count, model_width)
    attended_low = low(low_back(attended * alive_col))
    summed_one = tokens + low_back(matmul(attended_low, w_out) + b_out)
    normed_one = layer_norm(summed_one, gain_one, shift_one)
    inner = low_back(matmul(low(normed_one), w_in) + b_in)
    gated_low = low(smooth_gate(inner))
    summed_two = normed_one + low_back(matmul(gated_low, w_back) + b_back)
    return layer_norm(summed_two, gain_two, shift_two) * alive_col

def reference(hidden, cotangent, seq_lengths, w_qkv, b_qv, w_out, b_out, gain_one, shift_one, w_in, b_in, w_back, b_back, gain_two, shift_two):
    params = tuple((array.astype(jnp.float32) for array in (w_qkv, b_qv, w_out, b_out, gain_one, shift_one, w_in, b_in, w_back, b_back, gain_two, shift_two)))
    group = math.gcd(N_FSDP, max(1, 4096 // TOK_DEV))
    length_groups = seq_lengths.astype(jnp.int32).reshape(N_FSDP // group, group, BLK_DEV)

    def forward(tokens, weights):
        stacked = tokens.reshape(N_FSDP // group, group, TOK_DEV, D)

        def one_group(paired):
            return jax.vmap(lambda row_block, len_block: buffer_layer(row_block, len_block, weights))(paired[0], paired[1])
        mapped = lax.map(jax.checkpoint(one_group), (stacked, length_groups))
        return mapped.reshape(TOKENS, D)
    result, pullback = jax.vjp(forward, hidden.astype(jnp.float32), params)
    grad_tokens, grad_params = pullback(cotangent.astype(jnp.float32))
    return (result.astype(jnp.bfloat16), grad_tokens.astype(jnp.bfloat16), grad_params[0], grad_params[1], grad_params[2], grad_params[3], grad_params[4], grad_params[5], grad_params[6], grad_params[7], grad_params[8], grad_params[9], grad_params[10], grad_params[11])
```

```python
import functools

import jax
import jax.numpy as jnp
from jax import lax
from jax.experimental import pallas as pl
from jax.experimental.pallas import tpu as pltpu
from jax.sharding import PartitionSpec as P

HEAD_DIM = 64
MESH = pl.DeviceIdType.MESH
VMEM_LIMIT = 60 * 1024 * 1024


EPSILON = 1e-12


def chip_grid(count):
    chips = count // 2
    side = 1
    while 2 * side**3 < chips:
        side += 1
    if 2 * side**3 == chips:
        return side, 2 * side
    return 1, chips


class Place:
    def __init__(self, me, side, depth):
        self.me, self.side, self.depth = me, side, depth
        self.core = lax.rem(me, 2)
        chip = me // 2
        x, y = lax.rem(chip, side), lax.rem(chip // side, side)
        self.first = chip // (side * side)
        self.second = x + self.core * (y - x)
        self.third = y + self.core * (x - y)
        self.sibling = me + 1 - 2 * self.core

    def chip(self, de, db, da):
        return self.chip_for(self.core, self.first, self.second, self.third, de, db, da)

    def sibling_chip(self, de, db, da):
        return self.chip_for(1 - self.core, self.first, self.third, self.second, de, db, da)

    def chip_for(self, core, first, second, third, de, db, da):
        side = self.side
        one = lax.rem(first + de, self.depth)
        two = lax.rem(second + db, side)
        three = lax.rem(third + da, side)
        return (
            one * (side * side)
            + two * (1 + core * (side - 1))
            + three * (side - core * (side - 1))
        )

    def device(self, de, db, da):
        return 2 * self.chip(de, db, da) + self.core

    def partners(self):
        return (
            [self.device(0, 0, da) for da in range(1, self.side)]
            + [self.device(0, db, 0) for db in range(1, self.side)]
            + [self.device(de, 0, 0) for de in range(1, self.depth)]
            + [self.sibling]
        )


def greet(place):
    barrier = pltpu.get_barrier_semaphore()
    partners = place.partners()
    for partner in partners:
        pl.semaphore_signal(barrier, inc=1, device_id=(partner,), device_id_type=MESH)
    pl.semaphore_wait(barrier, len(partners))


def gather_kernel(side, depth, src, out, send_sem, recv_sem, own_sem):
    place = Place(lax.axis_index("fsdp"), side, depth)
    me, count = place.me, 2 * side * side * depth
    greet(place)
    own = pltpu.make_async_copy(src, out.at[me], own_sem)
    own.start()

    def send(block, slot, device, ticket):
        pltpu.make_async_remote_copy(
            src_ref=block,
            dst_ref=out.at[slot],
            send_sem=send_sem.at[ticket],
            recv_sem=recv_sem.at[slot],
            device_id=(device,),
            device_id_type=MESH,
        ).start()

    def arrive(slot):
        pltpu.make_async_copy(out.at[slot], out.at[slot], recv_sem.at[slot]).wait()

    for ticket, partner in enumerate(place.partners()):
        send(src, me, partner, ticket)
    base = 2 * (side - 1) + depth
    per_depth = side * side + side - 1

    def near(de, db, ticket):
        slot = place.device(de, db, 0)
        arrive(slot)
        for da in range(1, side):
            send(out.at[slot], slot, place.device(0, 0, da), ticket + da - 1)
        ticket = ticket + side - 1
        if db == 0:
            for other in range(1, side):
                send(out.at[slot], slot, place.device(0, other, 0), ticket + other - 1)
            ticket = ticket + side - 1
        send(out.at[slot], slot, place.sibling, ticket)
        return ticket + 1

    def far(de, ticket):
        for da in range(1, side):
            for db in range(side):
                slot = place.device(de, db, da)
                arrive(slot)
                send(out.at[slot], slot, place.sibling, ticket)
                ticket = ticket + 1
        return ticket

    ticket = base
    for db in range(1, side):
        ticket = near(0, db, ticket)
    start = ticket

    def step(de, carry):
        ticket = start + (de - 1) * (2 * side * side - 1)
        for db in range(side):
            ticket = near(de, db, ticket)
        far(de - 1, ticket)
        return carry

    lax.fori_loop(1, depth, step, 0)
    far(depth - 1, count - 1 - side * (side - 1))

    def from_sibling(chip, carry):
        arrive(2 * chip + 1 - place.core)
        return carry

    lax.fori_loop(0, count // 2, from_sibling, 0)
    own.wait()

    def sent(ticket, carry):
        pltpu.make_async_copy(src, src, send_sem.at[ticket]).wait()
        return carry

    lax.fori_loop(0, count - 1, sent, 0)


def gather_blocks(block, count):
    side, depth = chip_grid(count)
    return pl.pallas_call(
        functools.partial(gather_kernel, side, depth),
        out_shape=jax.ShapeDtypeStruct((count,) + block.shape, block.dtype),
        in_specs=[pl.BlockSpec(memory_space=pl.ANY)],
        out_specs=pl.BlockSpec(memory_space=pl.ANY),
        scratch_shapes=[
            pltpu.SemaphoreType.DMA((count,)),
            pltpu.SemaphoreType.DMA((count,)),
            pltpu.SemaphoreType.DMA,
        ],
        compiler_params=pltpu.CompilerParams(
            collective_id=0, has_side_effects=True, vmem_limit_bytes=VMEM_LIMIT
        ),
    )(block)


def scatter_kernel(
    side, depth, terms, out, pair, third, second, first, send_sem, pair_sem, third_sem, second_sem, first_sem
):
    place = Place(lax.axis_index("fsdp"), side, depth)
    core, chips = place.core, side * side * depth
    count = 2 * chips
    greet(place)

    def send(block, target, sem, device, ticket):
        pltpu.make_async_remote_copy(
            src_ref=block,
            dst_ref=target,
            send_sem=send_sem.at[ticket],
            recv_sem=sem,
            device_id=(device,),
            device_id_type=MESH,
        ).start()

    def arrive(block, sem):
        pltpu.make_async_copy(block, block, sem).wait()

    def wide(block):
        return block[...].astype(jnp.float32)

    def give(index, carry):
        da = lax.rem(index // (side * depth) + 1, side)
        de = lax.rem(lax.rem(index, side * depth) // side + 1, depth)
        db = lax.rem(lax.rem(index, side) + 1, side)
        chip = place.sibling_chip(de, db, da)
        send(terms.at[2 * chip + 1 - core], pair.at[chip], pair_sem.at[chip], place.sibling, chip)
        return carry

    lax.fori_loop(0, chips, give, 0)

    def outward(index, carry):
        da = index // (side * depth) + 1
        de = lax.rem(lax.rem(index, side * depth) // side + 1, depth)
        db = lax.rem(lax.rem(index, side) + 1, side)
        chip = place.chip(de, db, da)
        held = pair.at[chip]
        arrive(held, pair_sem.at[chip])
        held[...] = (wide(held) + wide(terms.at[2 * chip + core])).astype(held.dtype)
        slot = de * side + db
        send(
            held,
            third.at[side - 1 - da, slot],
            third_sem.at[side - 1 - da, slot],
            place.device(0, 0, da),
            chips + index,
        )
        return carry

    lax.fori_loop(0, chips - side * depth, outward, 0)
    base = 2 * chips - side * depth

    def along_second(de, ticket):
        for db in list(range(1, side)) + [0]:
            chip = place.chip(de, db, 0)
            held = pair.at[chip]
            arrive(held, pair_sem.at[chip])
            slot = de * side + db
            total = wide(held) + wide(terms.at[2 * chip + core])
            for other in range(side - 1):
                arrive(third.at[other, slot], third_sem.at[other, slot])
                total = total + wide(third.at[other, slot])
            held[...] = total.astype(held.dtype)
            if db > 0:
                send(
                    held,
                    second.at[side - 1 - db, de],
                    second_sem.at[side - 1 - db, de],
                    place.device(0, db, 0),
                    ticket + db - 1,
                )

    def second_total(de):
        held = pair.at[place.chip(de, 0, 0)]
        total = wide(held)
        for other in range(side - 1):
            arrive(second.at[other, de], second_sem.at[other, de])
            total = total + wide(second.at[other, de])
        return held, total

    def along_first(de):
        held, total = second_total(de)
        held[...] = total.astype(held.dtype)
        send(
            held,
            first.at[depth - 1 - de],
            first_sem.at[depth - 1 - de],
            place.device(de, 0, 0),
            count - 1 - de,
        )

    def step(index, carry):
        along_second(lax.rem(index, depth), base + (index - 1) * (side - 1))

        @pl.when(index > 1)
        def last():
            along_first(index - 1)

        return carry

    lax.fori_loop(1, depth + 1, step, 0)
    held, total = second_total(0)
    for other in range(depth - 1):
        arrive(first.at[other], first_sem.at[other])
        total = total + wide(first.at[other])
    out[...] = total

    def sent(ticket, carry):
        pltpu.make_async_copy(terms.at[0], terms.at[0], send_sem.at[ticket]).wait()
        return carry

    lax.fori_loop(0, count - 1, sent, 0)


def scatter_blocks(terms):
    count = terms.shape[0]
    side, depth = chip_grid(count)
    block = terms.shape[1:]
    chips = count // 2
    lanes = max(side - 1, 1)
    return pl.pallas_call(
        functools.partial(scatter_kernel, side, depth),
        out_shape=jax.ShapeDtypeStruct(block, jnp.float32),
        in_specs=[pl.BlockSpec(memory_space=pltpu.VMEM)],
        out_specs=pl.BlockSpec(memory_space=pltpu.VMEM),
        scratch_shapes=[
            pltpu.VMEM((chips,) + block, terms.dtype),
            pltpu.VMEM((lanes, side * depth) + block, terms.dtype),
            pltpu.VMEM((lanes, depth) + block, terms.dtype),
            pltpu.VMEM((depth - 1,) + block, terms.dtype),
            pltpu.SemaphoreType.DMA((count,)),
            pltpu.SemaphoreType.DMA((chips,)),
            pltpu.SemaphoreType.DMA((lanes, side * depth)),
            pltpu.SemaphoreType.DMA((lanes, depth)),
            pltpu.SemaphoreType.DMA((depth - 1,)),
        ],
        compiler_params=pltpu.CompilerParams(
            collective_id=1, has_side_effects=True, vmem_limit_bytes=VMEM_LIMIT
        ),
    )(terms)


def padded_rows(rows):
    return -(-rows // 16) * 16


def chunk_columns(weight, width):
    return jnp.concatenate(
        [weight[:, :, start : start + width] for start in range(0, weight.shape[2], width)], axis=1
    )


def pack(matrices, vectors, width, dtype):
    parts = [chunk_columns(matrix.astype(dtype), width) for matrix in matrices]
    line = jnp.concatenate([vector.astype(dtype) for vector in vectors], axis=1)
    rows = sum(part.shape[1] for part in parts)
    tail = padded_rows(rows + -(-line.shape[1] // width)) - rows
    line = jnp.pad(line, ((0, 0), (0, tail * width - line.shape[1])))
    return jnp.concatenate(parts + [line.reshape(line.shape[0], tail, width)], axis=1)


def unpack(blocks, matrix_shapes, vector_sizes):
    count, _, width = blocks.shape
    matrices, row = [], 0
    for rows, columns in matrix_shapes:
        chunks = []
        for _ in range(columns // width):
            chunks.append(blocks[:, row : row + rows, :].reshape(count * rows, width))
            row += rows
        matrices.append(jnp.concatenate(chunks, axis=1))
    line = blocks[:, row:, :].reshape(count, -1)
    vectors, place = [], 0
    for size in vector_sizes:
        vectors.append(line[:, place : place + size].reshape(count * size))
        place += size
    return matrices, vectors


def layer_norm(values, gain, shift):
    centre = values - jnp.mean(values, axis=-1, keepdims=True)
    spread = jnp.mean(centre * centre, axis=-1, keepdims=True)
    return centre * lax.rsqrt(spread + EPSILON) * gain + shift


def smooth_gate(values):
    return jax.nn.gelu(values, approximate=False)


def seq_masks(lengths, row_count):
    blocks = lengths.shape[0]
    block_width = row_count // blocks
    block_ids = jnp.arange(blocks, dtype=jnp.int32)
    starts = jnp.where(lengths > 0, block_ids, 0)
    owners = lax.cummax(starts, axis=0)
    position = jnp.arange(row_count, dtype=jnp.int32)
    member = position[:, None] // block_width == block_ids[None, :]
    owner_row = jnp.sum(jnp.where(member, owners[None, :], 0), axis=1)
    chosen = owner_row[:, None] == block_ids[None, :]
    length_row = jnp.sum(jnp.where(chosen, lengths[None, :], 0), axis=1)
    alive_row = position - owner_row * block_width < length_row
    same_seq = (owner_row[:, None] == owner_row[None, :]) & alive_row[None, :]
    return (alive_row, same_seq)


def outer_sum(left, right):
    return lax.dot_general(
        left, right, (((0,), (0,)), ((), ())), preferred_element_type=jnp.float32
    )


def column_term(left, right):
    return outer_sum(left, right)


def back_product(grad, weight):
    return lax.dot_general(
        grad, weight, (((1,), (1,)), ((), ())), preferred_element_type=jnp.float32
    )


def masked_scores(queries, keys_all, same_seq, factor):
    raw = jnp.einsum("qhd,khd->hqk", queries, keys_all, preferred_element_type=jnp.float32) * factor
    return jnp.where(same_seq[None], raw, -1e30)


def shards(
    hidden,
    cotangent,
    seq_lengths,
    w_qkv,
    b_qv,
    w_out,
    b_out,
    gain_one,
    shift_one,
    w_in,
    b_in,
    w_back,
    b_back,
    gain_two,
    shift_two,
):
    row_count, model_width = hidden.shape
    head_count = model_width // HEAD_DIM
    factor = HEAD_DIM ** (-0.5)
    alive_row, same_seq = seq_masks(seq_lengths, row_count)
    alive_col = alive_row.astype(jnp.float32)[:, None]
    count = lax.axis_size("fsdp")
    weights = (w_qkv, w_out, w_in, w_back)
    biases = (b_qv, b_out, gain_one, shift_one, b_in, b_back, gain_two, shift_two)
    weight_shapes = [weight.shape for weight in weights]
    bias_sizes = [bias.shape[0] for bias in biases]
    block = pack(
        [weight[None] for weight in weights],
        [bias[None] for bias in biases],
        model_width,
        jnp.bfloat16,
    )[0]
    (full_qkv, full_out, full_in, full_back), full_biases = unpack(
        gather_blocks(block, count), weight_shapes, bias_sizes
    )
    (
        full_bqv,
        full_bout,
        full_gone,
        full_sone,
        full_bin,
        full_bback,
        full_gtwo,
        full_stwo,
    ) = full_biases
    bias_qv = full_bqv.astype(jnp.float32)
    bias_qkv = jnp.concatenate(
        [bias_qv[:model_width], jnp.zeros((model_width,), jnp.float32), bias_qv[model_width:]]
    )
    qkv_low = (jnp.dot(hidden, full_qkv, preferred_element_type=jnp.float32) + bias_qkv).astype(
        jnp.bfloat16
    )
    queries = qkv_low[:, :model_width].reshape(row_count, head_count, HEAD_DIM)
    keys_all = qkv_low[:, model_width : 2 * model_width].reshape(row_count, head_count, HEAD_DIM)
    values_all = qkv_low[:, 2 * model_width :].reshape(row_count, head_count, HEAD_DIM)
    scores = masked_scores(queries, keys_all, same_seq, factor)
    highest = jnp.max(scores, axis=-1, keepdims=True)
    expo = jnp.exp(scores - highest)
    totals = jnp.sum(expo, axis=-1, keepdims=True)
    log_total = highest + jnp.log(totals)
    probs_low = (expo / totals).astype(jnp.bfloat16)
    attended = jnp.einsum(
        "hqk,khd->qhd", probs_low, values_all, preferred_element_type=jnp.float32
    ).reshape(row_count, model_width)
    attended_low = (attended * alive_col).astype(jnp.bfloat16)
    summed_one = (
        hidden.astype(jnp.float32)
        + jnp.dot(attended_low, full_out, preferred_element_type=jnp.float32)
        + full_bout.astype(jnp.float32)
    )
    normed_one = layer_norm(
        summed_one, full_gone.astype(jnp.float32), full_sone.astype(jnp.float32)
    )
    normed_low = normed_one.astype(jnp.bfloat16)
    inner = jnp.dot(normed_low, full_in, preferred_element_type=jnp.float32) + full_bin.astype(
        jnp.float32
    )
    gated_low = smooth_gate(inner).astype(jnp.bfloat16)
    summed_two = (
        normed_one
        + jnp.dot(gated_low, full_back, preferred_element_type=jnp.float32)
        + full_bback.astype(jnp.float32)
    )
    output = (
        layer_norm(summed_two, full_gtwo.astype(jnp.float32), full_stwo.astype(jnp.float32))
        * alive_col
    ).astype(jnp.bfloat16)
    shift_zero = jnp.zeros((model_width,), jnp.float32)
    unused, norm_two_back = jax.vjp(
        layer_norm, summed_two, full_gtwo.astype(jnp.float32), shift_zero
    )
    grad_sum_two, grad_gtwo, grad_stwo = norm_two_back(cotangent.astype(jnp.float32) * alive_col)
    grad_branch_two = grad_sum_two.astype(jnp.bfloat16)
    term_bback = jnp.sum(grad_branch_two.astype(jnp.float32), axis=0)
    grad_gated = back_product(grad_branch_two, full_back)
    unused, gate_back = jax.vjp(smooth_gate, inner)
    grad_inner = gate_back(grad_gated)[0].astype(jnp.bfloat16)
    term_bin = jnp.sum(grad_inner.astype(jnp.float32), axis=0)
    grad_normed = grad_sum_two + back_product(grad_inner, full_in)
    unused, norm_one_back = jax.vjp(
        layer_norm, summed_one, full_gone.astype(jnp.float32), shift_zero
    )
    grad_sum_one, grad_gone, grad_sone = norm_one_back(grad_normed)
    grad_branch_one = grad_sum_one.astype(jnp.bfloat16)
    term_bout = jnp.sum(grad_branch_one.astype(jnp.float32), axis=0)
    grad_attended = (
        (back_product(grad_branch_one, full_out) * alive_col)
        .astype(jnp.bfloat16)
        .reshape(row_count, head_count, HEAD_DIM)
    )
    scores_again = masked_scores(queries, keys_all, same_seq, factor)
    probs = jnp.exp(scores_again - log_total)
    probs_again_low = probs.astype(jnp.bfloat16)
    grad_probs = jnp.einsum(
        "qhd,khd->hqk", grad_attended, values_all, preferred_element_type=jnp.float32
    )
    inner_dot = jnp.sum(probs * grad_probs, axis=-1, keepdims=True)
    grad_scores = jnp.where(same_seq[None], probs * (grad_probs - inner_dot), 0.0).astype(
        jnp.bfloat16
    )
    grad_queries = (
        jnp.einsum("hqk,khd->qhd", grad_scores, keys_all, preferred_element_type=jnp.float32)
        * factor
    )
    grad_keys = (
        jnp.einsum("hqk,qhd->khd", grad_scores, queries, preferred_element_type=jnp.float32)
        * factor
    )
    grad_values = jnp.einsum(
        "hqk,qhd->khd", probs_again_low, grad_attended, preferred_element_type=jnp.float32
    )
    grad_qkv = jnp.concatenate(
        [
            grad_queries.reshape(row_count, model_width),
            grad_keys.reshape(row_count, model_width),
            grad_values.reshape(row_count, model_width),
        ],
        axis=1,
    ).astype(jnp.bfloat16)
    column_sums = jnp.sum(grad_qkv.astype(jnp.float32), axis=0)
    term_bqv = jnp.concatenate([column_sums[:model_width], column_sums[2 * model_width :]])
    grad_hidden = (grad_sum_one + back_product(grad_qkv, full_qkv)).astype(jnp.bfloat16)
    terms = pack(
        [
            column_term(left, right).reshape(count, -1, right.shape[1])
            for left, right in (
                (hidden, grad_qkv),
                (attended_low, grad_branch_one),
                (normed_low, grad_inner),
                (gated_low, grad_branch_two),
            )
        ],
        [
            vector.reshape(count, -1)
            for vector in (
                term_bqv,
                term_bout,
                grad_gone,
                grad_sone,
                term_bin,
                term_bback,
                grad_gtwo,
                grad_stwo,
            )
        ],
        model_width,
        jnp.bfloat16,
    )
    (share_qkv, share_out, share_in, share_back), vectors = unpack(
        scatter_blocks(terms)[None], weight_shapes, bias_sizes
    )
    return (
        output,
        grad_hidden,
        share_qkv,
        vectors[0],
        share_out,
        vectors[1],
        vectors[2],
        vectors[3],
        share_in,
        vectors[4],
        share_back,
        vectors[5],
        vectors[6],
        vectors[7],
    )


def solution(mesh):
    return jax.shard_map(
        shards,
        mesh=mesh,
        in_specs=(
            P("fsdp", None),
            P("fsdp", None),
            P("fsdp"),
            P("fsdp", None),
            P("fsdp"),
            P("fsdp", None),
            P("fsdp"),
            P("fsdp"),
            P("fsdp"),
            P("fsdp", None),
            P("fsdp"),
            P("fsdp", None),
            P("fsdp"),
            P("fsdp"),
            P("fsdp"),
        ),
        out_specs=(
            P("fsdp", None),
            P("fsdp", None),
            P("fsdp", None),
            P("fsdp"),
            P("fsdp", None),
            P("fsdp"),
            P("fsdp"),
            P("fsdp"),
            P("fsdp", None),
            P("fsdp"),
            P("fsdp", None),
            P("fsdp"),
            P("fsdp"),
            P("fsdp"),
        ),
        check_vma=False,
    )
```

```python
import functools

import jax
import jax.numpy as jnp
from jax import lax
from jax.experimental import pallas as pl
from jax.experimental.pallas import tpu as pltpu
from jax.sharding import PartitionSpec as P

HEAD_DIM = 64
MESH = pl.DeviceIdType.MESH
VMEM_LIMIT = 60 * 1024 * 1024


EPSILON = 1e-12


def chip_grid(count):
    chips = count // 2
    side = 1
    while 2 * side**3 < chips:
        side += 1
    if 2 * side**3 == chips:
        return side, 2 * side
    return 1, chips


class Place:
    def __init__(self, me, side, depth):
        self.me, self.side, self.depth = me, side, depth
        self.core = lax.rem(me, 2)
        chip = me // 2
        x, y = lax.rem(chip, side), lax.rem(chip // side, side)
        self.first = chip // (side * side)
        self.second = x + self.core * (y - x)
        self.third = y + self.core * (x - y)
        self.sibling = me + 1 - 2 * self.core

    def chip(self, de, db, da):
        return self.chip_for(self.core, self.first, self.second, self.third, de, db, da)

    def sibling_chip(self, de, db, da):
        return self.chip_for(1 - self.core, self.first, self.third, self.second, de, db, da)

    def chip_for(self, core, first, second, third, de, db, da):
        side = self.side
        one = lax.rem(first + de, self.depth)
        two = lax.rem(second + db, side)
        three = lax.rem(third + da, side)
        return (
            one * (side * side)
            + two * (1 + core * (side - 1))
            + three * (side - core * (side - 1))
        )

    def device(self, de, db, da):
        return 2 * self.chip(de, db, da) + self.core

    def partners(self):
        return (
            [self.device(0, 0, da) for da in range(1, self.side)]
            + [self.device(0, db, 0) for db in range(1, self.side)]
            + [self.device(de, 0, 0) for de in range(1, self.depth)]
            + [self.sibling]
        )


def greet(place):
    barrier = pltpu.get_barrier_semaphore()
    partners = place.partners()
    for partner in partners:
        pl.semaphore_signal(barrier, inc=1, device_id=(partner,), device_id_type=MESH)
    pl.semaphore_wait(barrier, len(partners))


def gather_kernel(side, depth, src, out, send_sem, recv_sem, own_sem):
    place = Place(lax.axis_index("fsdp"), side, depth)
    me, count = place.me, 2 * side * side * depth
    greet(place)
    own = pltpu.make_async_copy(src, out.at[me], own_sem)
    own.start()

    def send(block, slot, device, ticket):
        pltpu.make_async_remote_copy(
            src_ref=block,
            dst_ref=out.at[slot],
            send_sem=send_sem.at[ticket],
            recv_sem=recv_sem.at[slot],
            device_id=(device,),
            device_id_type=MESH,
        ).start()

    def arrive(slot):
        pltpu.make_async_copy(out.at[slot], out.at[slot], recv_sem.at[slot]).wait()

    for ticket, partner in enumerate(place.partners()):
        send(src, me, partner, ticket)
    base = 2 * (side - 1) + depth
    per_depth = side * side + side - 1

    def near(de, db, ticket):
        slot = place.device(de, db, 0)
        arrive(slot)
        for da in range(1, side):
            send(out.at[slot], slot, place.device(0, 0, da), ticket + da - 1)
        ticket = ticket + side - 1
        if db == 0:
            for other in range(1, side):
                send(out.at[slot], slot, place.device(0, other, 0), ticket + other - 1)
            ticket = ticket + side - 1
        send(out.at[slot], slot, place.sibling, ticket)
        return ticket + 1

    def far(de, ticket):
        for da in range(1, side):
            for db in range(side):
                slot = place.device(de, db, da)
                arrive(slot)
                send(out.at[slot], slot, place.sibling, ticket)
                ticket = ticket + 1
        return ticket

    ticket = base
    for db in range(1, side):
        ticket = near(0, db, ticket)
    start = ticket

    def step(de, carry):
        ticket = start + (de - 1) * (2 * side * side - 1)
        for db in range(side):
            ticket = near(de, db, ticket)
        far(de - 1, ticket)
        return carry

    lax.fori_loop(1, depth, step, 0)
    far(depth - 1, count - 1 - side * (side - 1))

    def from_sibling(chip, carry):
        arrive(2 * chip + 1 - place.core)
        return carry

    lax.fori_loop(0, count // 2, from_sibling, 0)
    own.wait()

    def sent(ticket, carry):
        pltpu.make_async_copy(src, src, send_sem.at[ticket]).wait()
        return carry

    lax.fori_loop(0, count - 1, sent, 0)


def gather_blocks(block, count):
    side, depth = chip_grid(count)
    return pl.pallas_call(
        functools.partial(gather_kernel, side, depth),
        out_shape=jax.ShapeDtypeStruct((count,) + block.shape, block.dtype),
        in_specs=[pl.BlockSpec(memory_space=pl.ANY)],
        out_specs=pl.BlockSpec(memory_space=pl.ANY),
        scratch_shapes=[
            pltpu.SemaphoreType.DMA((count,)),
            pltpu.SemaphoreType.DMA((count,)),
            pltpu.SemaphoreType.DMA,
        ],
        compiler_params=pltpu.CompilerParams(
            collective_id=0, has_side_effects=True, vmem_limit_bytes=VMEM_LIMIT
        ),
    )(block)


def scatter_kernel(
    side, depth, terms, out, pair, third, second, first, send_sem, pair_sem, third_sem, second_sem, first_sem
):
    place = Place(lax.axis_index("fsdp"), side, depth)
    core, chips = place.core, side * side * depth
    count = 2 * chips
    greet(place)

    def send(block, target, sem, device, ticket):
        pltpu.make_async_remote_copy(
            src_ref=block,
            dst_ref=target,
            send_sem=send_sem.at[ticket],
            recv_sem=sem,
            device_id=(device,),
            device_id_type=MESH,
        ).start()

    def arrive(block, sem):
        pltpu.make_async_copy(block, block, sem).wait()

    def wide(block):
        return block[...].astype(jnp.float32)

    def give(index, carry):
        da = lax.rem(index // (side * depth) + 1, side)
        de = lax.rem(lax.rem(index, side * depth) // side + 1, depth)
        db = lax.rem(lax.rem(index, side) + 1, side)
        chip = place.sibling_chip(de, db, da)
        send(terms.at[2 * chip + 1 - core], pair.at[chip], pair_sem.at[chip], place.sibling, chip)
        return carry

    lax.fori_loop(0, chips, give, 0)

    def outward(index, carry):
        da = index // (side * depth) + 1
        de = lax.rem(lax.rem(index, side * depth) // side + 1, depth)
        db = lax.rem(lax.rem(index, side) + 1, side)
        chip = place.chip(de, db, da)
        held = pair.at[chip]
        arrive(held, pair_sem.at[chip])
        held[...] = (wide(held) + wide(terms.at[2 * chip + core])).astype(held.dtype)
        slot = de * side + db
        send(
            held,
            third.at[side - 1 - da, slot],
            third_sem.at[side - 1 - da, slot],
            place.device(0, 0, da),
            chips + index,
        )
        return carry

    lax.fori_loop(0, chips - side * depth, outward, 0)
    base = 2 * chips - side * depth

    def along_second(de, ticket):
        for db in list(range(1, side)) + [0]:
            chip = place.chip(de, db, 0)
            held = pair.at[chip]
            arrive(held, pair_sem.at[chip])
            slot = de * side + db
            total = wide(held) + wide(terms.at[2 * chip + core])
            for other in range(side - 1):
                arrive(third.at[other, slot], third_sem.at[other, slot])
                total = total + wide(third.at[other, slot])
            held[...] = total.astype(held.dtype)
            if db > 0:
                send(
                    held,
                    second.at[side - 1 - db, de],
                    second_sem.at[side - 1 - db, de],
                    place.device(0, db, 0),
                    ticket + db - 1,
                )

    def second_total(de):
        held = pair.at[place.chip(de, 0, 0)]
        total = wide(held)
        for other in range(side - 1):
            arrive(second.at[other, de], second_sem.at[other, de])
            total = total + wide(second.at[other, de])
        return held, total

    def along_first(de):
        held, total = second_total(de)
        held[...] = total.astype(held.dtype)
        send(
            held,
            first.at[depth - 1 - de],
            first_sem.at[depth - 1 - de],
            place.device(de, 0, 0),
            count - 1 - de,
        )

    def step(index, carry):
        along_second(lax.rem(index, depth), base + (index - 1) * (side - 1))

        @pl.when(index > 1)
        def last():
            along_first(index - 1)

        return carry

    lax.fori_loop(1, depth + 1, step, 0)
    held, total = second_total(0)
    for other in range(depth - 1):
        arrive(first.at[other], first_sem.at[other])
        total = total + wide(first.at[other])
    out[...] = total

    def sent(ticket, carry):
        pltpu.make_async_copy(terms.at[0], terms.at[0], send_sem.at[ticket]).wait()
        return carry

    lax.fori_loop(0, count - 1, sent, 0)


def scatter_blocks(terms):
    count = terms.shape[0]
    side, depth = chip_grid(count)
    block = terms.shape[1:]
    chips = count // 2
    lanes = max(side - 1, 1)
    return pl.pallas_call(
        functools.partial(scatter_kernel, side, depth),
        out_shape=jax.ShapeDtypeStruct(block, jnp.float32),
        in_specs=[pl.BlockSpec(memory_space=pltpu.VMEM)],
        out_specs=pl.BlockSpec(memory_space=pltpu.VMEM),
        scratch_shapes=[
            pltpu.VMEM((chips,) + block, terms.dtype),
            pltpu.VMEM((lanes, side * depth) + block, terms.dtype),
            pltpu.VMEM((lanes, depth) + block, terms.dtype),
            pltpu.VMEM((depth - 1,) + block, terms.dtype),
            pltpu.SemaphoreType.DMA((count,)),
            pltpu.SemaphoreType.DMA((chips,)),
            pltpu.SemaphoreType.DMA((lanes, side * depth)),
            pltpu.SemaphoreType.DMA((lanes, depth)),
            pltpu.SemaphoreType.DMA((depth - 1,)),
        ],
        compiler_params=pltpu.CompilerParams(
            collective_id=1, has_side_effects=True, vmem_limit_bytes=VMEM_LIMIT
        ),
    )(terms)


def padded_rows(rows):
    return -(-rows // 16) * 16


def chunk_columns(weight, width):
    return jnp.concatenate(
        [weight[:, :, start : start + width] for start in range(0, weight.shape[2], width)], axis=1
    )


def pack(matrices, vectors, width, dtype):
    parts = [chunk_columns(matrix.astype(dtype), width) for matrix in matrices]
    line = jnp.concatenate([vector.astype(dtype) for vector in vectors], axis=1)
    rows = sum(part.shape[1] for part in parts)
    tail = padded_rows(rows + -(-line.shape[1] // width)) - rows
    line = jnp.pad(line, ((0, 0), (0, tail * width - line.shape[1])))
    return jnp.concatenate(parts + [line.reshape(line.shape[0], tail, width)], axis=1)


def unpack(blocks, matrix_shapes, vector_sizes):
    count, _, width = blocks.shape
    matrices, row = [], 0
    for rows, columns in matrix_shapes:
        chunks = []
        for _ in range(columns // width):
            chunks.append(blocks[:, row : row + rows, :].reshape(count * rows, width))
            row += rows
        matrices.append(jnp.concatenate(chunks, axis=1))
    line = blocks[:, row:, :].reshape(count, -1)
    vectors, place = [], 0
    for size in vector_sizes:
        vectors.append(line[:, place : place + size].reshape(count * size))
        place += size
    return matrices, vectors


def seq_masks(lengths, row_count):
    blocks = lengths.shape[0]
    block_width = row_count // blocks
    block_ids = jnp.arange(blocks, dtype=jnp.int32)
    starts = jnp.where(lengths > 0, block_ids, 0)
    owners = lax.cummax(starts, axis=0)
    position = jnp.arange(row_count, dtype=jnp.int32)
    member = position[:, None] // block_width == block_ids[None, :]
    owner_row = jnp.sum(jnp.where(member, owners[None, :], 0), axis=1)
    chosen = owner_row[:, None] == block_ids[None, :]
    length_row = jnp.sum(jnp.where(chosen, lengths[None, :], 0), axis=1)
    alive_row = position - owner_row * block_width < length_row
    same_seq = (owner_row[:, None] == owner_row[None, :]) & alive_row[None, :]
    return (alive_row, same_seq)


def outer_sum(left, right):
    return lax.dot_general(
        left, right, (((0,), (0,)), ((), ())), preferred_element_type=jnp.float32
    )


def back_product(grad, weight):
    return lax.dot_general(
        grad, weight, (((1,), (1,)), ((), ())), preferred_element_type=jnp.float32
    )


def matmul(left, right):
    return jnp.dot(left, right, preferred_element_type=jnp.float32)


def column_sum(values):
    return jnp.sum(values, axis=0, keepdims=True)


def row_mean(values):
    return jnp.mean(values, axis=-1, keepdims=True)


def normalise(values):
    centre = values - row_mean(values)
    scale = lax.rsqrt(row_mean(centre * centre) + EPSILON)
    return centre * scale, scale


def norm_back(grad, gain, unit, scale):
    scaled = grad * gain
    return scale * (scaled - row_mean(scaled) - unit * row_mean(scaled * unit))


def layer_kernel(
    hidden_ref,
    cotangent_ref,
    alive_ref,
    same_ref,
    w_qkv,
    w_out,
    w_in,
    w_back,
    bias_qkv,
    b_out,
    gain_one,
    shift_one,
    b_in,
    b_back,
    gain_two,
    shift_two,
    output_ref,
    grad_hidden_ref,
    dw_qkv,
    dw_out,
    dw_in,
    dw_back,
    db_qkv,
    db_out,
    dgain_one,
    dshift_one,
    db_in,
    db_back,
    dgain_two,
    dshift_two,
    qkv_ref,
    probs_ref,
    attended_ref,
    unit_one_ref,
    gated_ref,
    slope_ref,
    grad_sum_ref,
    grad_attended_ref,
    grad_qkv_ref,
):
    low, wide = jnp.bfloat16, jnp.float32
    rows, width = hidden_ref.shape
    factor = HEAD_DIM ** (-0.5)
    pair_width = 2 * HEAD_DIM
    alive = alive_ref[...]
    hidden_width = w_in.shape[1]
    spans = [slice(start, start + width) for start in range(0, hidden_width, width)]
    left_half = lax.broadcasted_iota(jnp.int32, (rows, pair_width), 1) < HEAD_DIM

    for part in range(3):
        span = slice(part * width, (part + 1) * width)
        projected = matmul(hidden_ref[...], w_qkv[:, span]) + bias_qkv[:, span]
        if part == 0:
            projected = projected * factor
        qkv_ref[:, span] = projected.astype(low)

    def pair_span(part, pair):
        start = part * width + pair * pair_width
        return slice(start, start + pair_width)

    def halves(values):
        zero = jnp.zeros_like(values)
        return jnp.where(left_half, values, zero), jnp.where(left_half, zero, values)

    pairs = width // pair_width
    for pair in range(pairs):
        queries = qkv_ref[:, pair_span(0, pair)]
        keys = qkv_ref[:, pair_span(1, pair)]
        values = qkv_ref[:, pair_span(2, pair)]
        found = []
        for half, part in enumerate(halves(queries)):
            scores = jnp.where(same_ref[...] > 0, back_product(part, keys), -1e30)
            expo = jnp.exp(scores - jnp.max(scores, axis=-1, keepdims=True))
            probs = expo * (1.0 / jnp.sum(expo, axis=-1, keepdims=True))
            probs_ref[2 * pair + half] = probs
            found.append(matmul(probs.astype(low), values))
        attended = jnp.where(left_half, found[0], found[1]) * alive
        attended_ref[:, pair_span(0, pair)] = attended.astype(low)

    summed_one = hidden_ref[...].astype(wide) + matmul(attended_ref[...], w_out[...]) + b_out[...]
    unit_one, scale_one = normalise(summed_one)
    unit_one_ref[...] = unit_one
    normed_one = unit_one * gain_one[...] + shift_one[...]
    normed_low = normed_one.astype(low)
    summed_two = normed_one + b_back[...]
    for span in spans:
        inner = matmul(normed_low, w_in[:, span]) + b_in[:, span]
        below = 0.5 + 0.5 * lax.erf(inner * 0.7071067811865476)
        slope_ref[:, span] = below + inner * (0.3989422804014327 * jnp.exp(-0.5 * inner * inner))
        gated = (inner * below).astype(low)
        gated_ref[:, span] = gated
        summed_two = summed_two + matmul(gated, w_back[span, :])
    unit_two, scale_two = normalise(summed_two)
    output_ref[...] = ((unit_two * gain_two[...] + shift_two[...]) * alive).astype(low)

    grad_out = cotangent_ref[...].astype(wide) * alive
    dgain_two[...] = column_sum(grad_out * unit_two)
    dshift_two[...] = column_sum(grad_out)
    grad_sum_two = norm_back(grad_out, gain_two[...], unit_two, scale_two)
    branch_two = grad_sum_two.astype(low)
    db_back[...] = column_sum(branch_two.astype(wide))
    grad_normed = grad_sum_two
    for span in spans:
        dw_back[span, :] = outer_sum(gated_ref[:, span], branch_two).astype(low)
        grad_inner = (back_product(branch_two, w_back[span, :]) * slope_ref[:, span]).astype(low)
        db_in[:, span] = column_sum(grad_inner.astype(wide))
        dw_in[:, span] = outer_sum(normed_low, grad_inner).astype(low)
        grad_normed = grad_normed + back_product(grad_inner, w_in[:, span])
    unit_one = unit_one_ref[...]
    dgain_one[...] = column_sum(grad_normed * unit_one)
    dshift_one[...] = column_sum(grad_normed)
    grad_sum_one = norm_back(grad_normed, gain_one[...], unit_one, scale_one)
    grad_sum_ref[...] = grad_sum_one
    branch_one = grad_sum_one.astype(low)
    db_out[...] = column_sum(branch_one.astype(wide))
    dw_out[...] = outer_sum(attended_ref[...], branch_one).astype(low)
    grad_attended_ref[...] = (back_product(branch_one, w_out[...]) * alive).astype(low)

    for pair in range(pairs):
        queries = qkv_ref[:, pair_span(0, pair)]
        keys = qkv_ref[:, pair_span(1, pair)]
        values = qkv_ref[:, pair_span(2, pair)]
        grad_attended = grad_attended_ref[:, pair_span(0, pair)]
        found = []
        for half, part in enumerate(halves(grad_attended)):
            probs = probs_ref[2 * pair + half]
            grad_probs = back_product(part, values)
            inner_dot = jnp.sum(probs * grad_probs, axis=-1, keepdims=True)
            grad_scores = (probs * (grad_probs - inner_dot)).astype(low)
            found.append(
                (
                    matmul(grad_scores, keys) * factor,
                    outer_sum(grad_scores, queries),
                    outer_sum(probs.astype(low), grad_attended),
                )
            )
        for part in range(3):
            joined = jnp.where(left_half, found[0][part], found[1][part])
            grad_qkv_ref[:, pair_span(part, pair)] = joined.astype(low)

    grad_hidden = grad_sum_ref[...]
    for part in range(3):
        span = slice(part * width, (part + 1) * width)
        grad_part = grad_qkv_ref[:, span]
        db_qkv[:, span] = column_sum(grad_part.astype(wide))
        dw_qkv[:, span] = outer_sum(hidden_ref[...], grad_part).astype(low)
        grad_hidden = grad_hidden + back_product(grad_part, w_qkv[:, span])
    grad_hidden_ref[...] = grad_hidden.astype(low)


def layer(hidden, cotangent, alive, same, weights, lines):
    rows, width = hidden.shape
    heads, hidden_width = width // HEAD_DIM, weights[2].shape[1]
    low, wide = jnp.bfloat16, jnp.float32
    shape = jax.ShapeDtypeStruct
    outs = (
        [shape(hidden.shape, low)] * 2
        + [shape(weight.shape, low) for weight in weights]
        + [shape(line.shape, wide) for line in lines]
    )
    return pl.pallas_call(
        layer_kernel,
        out_shape=outs,
        in_specs=[pl.BlockSpec(memory_space=pltpu.VMEM)] * (4 + len(weights) + len(lines)),
        out_specs=[pl.BlockSpec(memory_space=pltpu.VMEM)] * len(outs),
        scratch_shapes=[
            pltpu.VMEM((rows, 3 * width), low),
            pltpu.VMEM((heads, rows, rows), wide),
            pltpu.VMEM((rows, width), low),
            pltpu.VMEM((rows, width), wide),
            pltpu.VMEM((rows, hidden_width), low),
            pltpu.VMEM((rows, hidden_width), wide),
            pltpu.VMEM((rows, width), wide),
            pltpu.VMEM((rows, width), low),
            pltpu.VMEM((rows, 3 * width), low),
        ],
        compiler_params=pltpu.CompilerParams(vmem_limit_bytes=VMEM_LIMIT),
    )(hidden, cotangent, alive, same, *weights, *lines)


def shards(
    hidden,
    cotangent,
    seq_lengths,
    w_qkv,
    b_qv,
    w_out,
    b_out,
    gain_one,
    shift_one,
    w_in,
    b_in,
    w_back,
    b_back,
    gain_two,
    shift_two,
):
    row_count, model_width = hidden.shape
    alive_row, same_seq = seq_masks(seq_lengths, row_count)
    alive_col = alive_row.astype(jnp.float32)[:, None]
    count = lax.axis_size("fsdp")
    weights = (w_qkv, w_out, w_in, w_back)
    biases = (b_qv, b_out, gain_one, shift_one, b_in, b_back, gain_two, shift_two)
    weight_shapes = [weight.shape for weight in weights]
    bias_sizes = [bias.shape[0] for bias in biases]
    block = pack(
        [weight[None] for weight in weights],
        [bias[None] for bias in biases],
        model_width,
        jnp.bfloat16,
    )[0]
    (full_qkv, full_out, full_in, full_back), full_biases = unpack(
        gather_blocks(block, count), weight_shapes, bias_sizes
    )
    (
        full_bqv,
        full_bout,
        full_gone,
        full_sone,
        full_bin,
        full_bback,
        full_gtwo,
        full_stwo,
    ) = full_biases
    bias_qkv = jnp.concatenate(
        [
            full_bqv[:model_width],
            jnp.zeros((model_width,), full_bqv.dtype),
            full_bqv[model_width:],
        ]
    )
    lines = [
        line.astype(jnp.float32)[None]
        for line in (
            bias_qkv,
            full_bout,
            full_gone,
            full_sone,
            full_bin,
            full_bback,
            full_gtwo,
            full_stwo,
        )
    ]
    results = layer(
        hidden,
        cotangent,
        alive_col,
        same_seq.astype(jnp.float32),
        (full_qkv, full_out, full_in, full_back),
        lines,
    )
    output, grad_hidden = results[:2]
    weight_terms, line_terms = results[2:6], [line[0] for line in results[6:]]
    line_terms[0] = jnp.concatenate(
        [line_terms[0][:model_width], line_terms[0][2 * model_width :]]
    )
    terms = pack(
        [term.reshape(count, -1, term.shape[1]) for term in weight_terms],
        [line.reshape(count, -1) for line in line_terms],
        model_width,
        jnp.bfloat16,
    )
    (share_qkv, share_out, share_in, share_back), vectors = unpack(
        scatter_blocks(terms)[None], weight_shapes, bias_sizes
    )
    return (
        output,
        grad_hidden,
        share_qkv,
        vectors[0],
        share_out,
        vectors[1],
        vectors[2],
        vectors[3],
        share_in,
        vectors[4],
        share_back,
        vectors[5],
        vectors[6],
        vectors[7],
    )


def solution(mesh):
    return jax.shard_map(
        shards,
        mesh=mesh,
        in_specs=(
            P("fsdp", None),
            P("fsdp", None),
            P("fsdp"),
            P("fsdp", None),
            P("fsdp"),
            P("fsdp", None),
            P("fsdp"),
            P("fsdp"),
            P("fsdp"),
            P("fsdp", None),
            P("fsdp"),
            P("fsdp", None),
            P("fsdp"),
            P("fsdp"),
            P("fsdp"),
        ),
        out_specs=(
            P("fsdp", None),
            P("fsdp", None),
            P("fsdp", None),
            P("fsdp"),
            P("fsdp", None),
            P("fsdp"),
            P("fsdp"),
            P("fsdp"),
            P("fsdp", None),
            P("fsdp"),
            P("fsdp", None),
            P("fsdp"),
            P("fsdp"),
            P("fsdp"),
        ),
        check_vma=False,
    )
```

```python
import functools

import jax
import jax.numpy as jnp
from jax import lax
from jax.experimental import pallas as pl
from jax.experimental.pallas import tpu as pltpu
from jax.sharding import PartitionSpec as P

HEAD_DIM = 64
MESH = pl.DeviceIdType.MESH
VMEM_LIMIT = 60 * 1024 * 1024


EPSILON = 1e-12


def chip_grid(count):
    chips = count // 2
    side = 1
    while 2 * side**3 < chips:
        side += 1
    if 2 * side**3 == chips:
        return side, 2 * side
    return 1, chips


class Place:
    def __init__(self, me, side, depth):
        self.me, self.side, self.depth = me, side, depth
        self.core = lax.rem(me, 2)
        chip = me // 2
        x, y = lax.rem(chip, side), lax.rem(chip // side, side)
        self.first = chip // (side * side)
        self.second = x + self.core * (y - x)
        self.third = y + self.core * (x - y)
        self.sibling = me + 1 - 2 * self.core

    def chip(self, de, db, da):
        return self.chip_for(self.core, self.first, self.second, self.third, de, db, da)

    def sibling_chip(self, de, db, da):
        return self.chip_for(1 - self.core, self.first, self.third, self.second, de, db, da)

    def chip_for(self, core, first, second, third, de, db, da):
        side = self.side
        one = lax.rem(first + de, self.depth)
        two = lax.rem(second + db, side)
        three = lax.rem(third + da, side)
        return (
            one * (side * side)
            + two * (1 + core * (side - 1))
            + three * (side - core * (side - 1))
        )

    def device(self, de, db, da):
        return 2 * self.chip(de, db, da) + self.core

    def partners(self):
        return (
            [self.device(0, 0, da) for da in range(1, self.side)]
            + [self.device(0, db, 0) for db in range(1, self.side)]
            + [self.device(de, 0, 0) for de in range(1, self.depth)]
            + [self.sibling]
        )


def greet(place):
    barrier = pltpu.get_barrier_semaphore()
    partners = place.partners()
    for partner in partners:
        pl.semaphore_signal(barrier, inc=1, device_id=(partner,), device_id_type=MESH)
    pl.semaphore_wait(barrier, len(partners))


def gather_kernel(side, depth, src, out, send_sem, recv_sem, own_sem):
    place = Place(lax.axis_index("fsdp"), side, depth)
    me, count = place.me, 2 * side * side * depth
    greet(place)
    own = pltpu.make_async_copy(src, out.at[me], own_sem)
    own.start()

    def send(block, slot, device, ticket):
        pltpu.make_async_remote_copy(
            src_ref=block,
            dst_ref=out.at[slot],
            send_sem=send_sem.at[ticket],
            recv_sem=recv_sem.at[slot],
            device_id=(device,),
            device_id_type=MESH,
        ).start()

    def arrive(slot):
        pltpu.make_async_copy(out.at[slot], out.at[slot], recv_sem.at[slot]).wait()

    for ticket, partner in enumerate(place.partners()):
        send(src, me, partner, ticket)
    base = 2 * (side - 1) + depth
    per_depth = side * side + side - 1

    def near(de, db, ticket):
        slot = place.device(de, db, 0)
        arrive(slot)
        for da in range(1, side):
            send(out.at[slot], slot, place.device(0, 0, da), ticket + da - 1)
        ticket = ticket + side - 1
        if db == 0:
            for other in range(1, side):
                send(out.at[slot], slot, place.device(0, other, 0), ticket + other - 1)
            ticket = ticket + side - 1
        send(out.at[slot], slot, place.sibling, ticket)
        return ticket + 1

    def far(de, ticket):
        for da in range(1, side):
            for db in range(side):
                slot = place.device(de, db, da)
                arrive(slot)
                send(out.at[slot], slot, place.sibling, ticket)
                ticket = ticket + 1
        return ticket

    ticket = base
    for db in range(1, side):
        ticket = near(0, db, ticket)
    start = ticket

    def step(de, carry):
        ticket = start + (de - 1) * (2 * side * side - 1)
        for db in range(side):
            ticket = near(de, db, ticket)
        far(de - 1, ticket)
        return carry

    lax.fori_loop(1, depth, step, 0)
    far(depth - 1, count - 1 - side * (side - 1))

    def from_sibling(chip, carry):
        arrive(2 * chip + 1 - place.core)
        return carry

    lax.fori_loop(0, count // 2, from_sibling, 0)
    own.wait()

    def sent(ticket, carry):
        pltpu.make_async_copy(src, src, send_sem.at[ticket]).wait()
        return carry

    lax.fori_loop(0, count - 1, sent, 0)


def gather_blocks(block, count):
    side, depth = chip_grid(count)
    return pl.pallas_call(
        functools.partial(gather_kernel, side, depth),
        out_shape=jax.ShapeDtypeStruct((count,) + block.shape, block.dtype),
        in_specs=[pl.BlockSpec(memory_space=pl.ANY)],
        out_specs=pl.BlockSpec(memory_space=pl.ANY),
        scratch_shapes=[
            pltpu.SemaphoreType.DMA((count,)),
            pltpu.SemaphoreType.DMA((count,)),
            pltpu.SemaphoreType.DMA,
        ],
        compiler_params=pltpu.CompilerParams(
            collective_id=0, has_side_effects=True, vmem_limit_bytes=VMEM_LIMIT
        ),
    )(block)


def scatter_kernel(
    side, depth, terms, out, pair, third, second, first, send_sem, pair_sem, third_sem, second_sem, first_sem
):
    place = Place(lax.axis_index("fsdp"), side, depth)
    core, chips = place.core, side * side * depth
    count = 2 * chips
    greet(place)

    def send(block, target, sem, device, ticket):
        pltpu.make_async_remote_copy(
            src_ref=block,
            dst_ref=target,
            send_sem=send_sem.at[ticket],
            recv_sem=sem,
            device_id=(device,),
            device_id_type=MESH,
        ).start()

    def arrive(block, sem):
        pltpu.make_async_copy(block, block, sem).wait()

    def wide(block):
        return block[...].astype(jnp.float32)

    def give(index, carry):
        da = lax.rem(index // (side * depth) + 1, side)
        de = lax.rem(lax.rem(index, side * depth) // side + 1, depth)
        db = lax.rem(lax.rem(index, side) + 1, side)
        chip = place.sibling_chip(de, db, da)
        send(terms.at[2 * chip + 1 - core], pair.at[chip], pair_sem.at[chip], place.sibling, chip)
        return carry

    lax.fori_loop(0, chips, give, 0)

    def outward(index, carry):
        da = index // (side * depth) + 1
        de = lax.rem(lax.rem(index, side * depth) // side + 1, depth)
        db = lax.rem(lax.rem(index, side) + 1, side)
        chip = place.chip(de, db, da)
        held = pair.at[chip]
        arrive(held, pair_sem.at[chip])
        held[...] = (wide(held) + wide(terms.at[2 * chip + core])).astype(held.dtype)
        slot = de * side + db
        send(
            held,
            third.at[side - 1 - da, slot],
            third_sem.at[side - 1 - da, slot],
            place.device(0, 0, da),
            chips + index,
        )
        return carry

    lax.fori_loop(0, chips - side * depth, outward, 0)
    base = 2 * chips - side * depth

    def along_second(de, ticket):
        for db in list(range(1, side)) + [0]:
            chip = place.chip(de, db, 0)
            held = pair.at[chip]
            arrive(held, pair_sem.at[chip])
            slot = de * side + db
            total = wide(held) + wide(terms.at[2 * chip + core])
            for other in range(side - 1):
                arrive(third.at[other, slot], third_sem.at[other, slot])
                total = total + wide(third.at[other, slot])
            held[...] = total.astype(held.dtype)
            if db > 0:
                send(
                    held,
                    second.at[side - 1 - db, de],
                    second_sem.at[side - 1 - db, de],
                    place.device(0, db, 0),
                    ticket + db - 1,
                )

    def second_total(de):
        held = pair.at[place.chip(de, 0, 0)]
        total = wide(held)
        for other in range(side - 1):
            arrive(second.at[other, de], second_sem.at[other, de])
            total = total + wide(second.at[other, de])
        return held, total

    def along_first(de):
        held, total = second_total(de)
        held[...] = total.astype(held.dtype)
        send(
            held,
            first.at[depth - 1 - de],
            first_sem.at[depth - 1 - de],
            place.device(de, 0, 0),
            count - 1 - de,
        )

    def step(index, carry):
        along_second(lax.rem(index, depth), base + (index - 1) * (side - 1))

        @pl.when(index > 1)
        def last():
            along_first(index - 1)

        return carry

    lax.fori_loop(1, depth + 1, step, 0)
    held, total = second_total(0)
    for other in range(depth - 1):
        arrive(first.at[other], first_sem.at[other])
        total = total + wide(first.at[other])
    out[...] = total

    def sent(ticket, carry):
        pltpu.make_async_copy(terms.at[0], terms.at[0], send_sem.at[ticket]).wait()
        return carry

    lax.fori_loop(0, count - 1, sent, 0)


def scatter_blocks(terms):
    count = terms.shape[0]
    side, depth = chip_grid(count)
    block = terms.shape[1:]
    chips = count // 2
    lanes = max(side - 1, 1)
    return pl.pallas_call(
        functools.partial(scatter_kernel, side, depth),
        out_shape=jax.ShapeDtypeStruct(block, jnp.float32),
        in_specs=[pl.BlockSpec(memory_space=pltpu.VMEM)],
        out_specs=pl.BlockSpec(memory_space=pltpu.VMEM),
        scratch_shapes=[
            pltpu.VMEM((chips,) + block, terms.dtype),
            pltpu.VMEM((lanes, side * depth) + block, terms.dtype),
            pltpu.VMEM((lanes, depth) + block, terms.dtype),
            pltpu.VMEM((depth - 1,) + block, terms.dtype),
            pltpu.SemaphoreType.DMA((count,)),
            pltpu.SemaphoreType.DMA((chips,)),
            pltpu.SemaphoreType.DMA((lanes, side * depth)),
            pltpu.SemaphoreType.DMA((lanes, depth)),
            pltpu.SemaphoreType.DMA((depth - 1,)),
        ],
        compiler_params=pltpu.CompilerParams(
            collective_id=1, has_side_effects=True, vmem_limit_bytes=VMEM_LIMIT
        ),
    )(terms)


def padded_rows(rows):
    return -(-rows // 16) * 16


def chunk_columns(weight, width):
    return jnp.concatenate(
        [weight[:, :, start : start + width] for start in range(0, weight.shape[2], width)], axis=1
    )


def pack(matrices, vectors, width, dtype):
    parts = [chunk_columns(matrix.astype(dtype), width) for matrix in matrices]
    line = jnp.concatenate([vector.astype(dtype) for vector in vectors], axis=1)
    rows = sum(part.shape[1] for part in parts)
    tail = padded_rows(rows + -(-line.shape[1] // width)) - rows
    line = jnp.pad(line, ((0, 0), (0, tail * width - line.shape[1])))
    return jnp.concatenate(parts + [line.reshape(line.shape[0], tail, width)], axis=1)


def unpack(blocks, matrix_shapes, vector_sizes):
    count, _, width = blocks.shape
    matrices, row = [], 0
    for rows, columns in matrix_shapes:
        chunks = []
        for _ in range(columns // width):
            chunks.append(blocks[:, row : row + rows, :].reshape(count * rows, width))
            row += rows
        matrices.append(jnp.concatenate(chunks, axis=1))
    line = blocks[:, row:, :].reshape(count, -1)
    vectors, place = [], 0
    for size in vector_sizes:
        vectors.append(line[:, place : place + size].reshape(count * size))
        place += size
    return matrices, vectors


def seq_masks(lengths, row_count):
    blocks = lengths.shape[0]
    block_width = row_count // blocks
    block_ids = jnp.arange(blocks, dtype=jnp.int32)
    starts = jnp.where(lengths > 0, block_ids, 0)
    owners = lax.cummax(starts, axis=0)
    position = jnp.arange(row_count, dtype=jnp.int32)
    member = position[:, None] // block_width == block_ids[None, :]
    owner_row = jnp.sum(jnp.where(member, owners[None, :], 0), axis=1)
    chosen = owner_row[:, None] == block_ids[None, :]
    length_row = jnp.sum(jnp.where(chosen, lengths[None, :], 0), axis=1)
    alive_row = position - owner_row * block_width < length_row
    same_seq = (owner_row[:, None] == owner_row[None, :]) & alive_row[None, :]
    return (alive_row, same_seq)


def outer_sum(left, right):
    return lax.dot_general(
        left, right, (((0,), (0,)), ((), ())), preferred_element_type=jnp.float32
    )


def back_product(grad, weight):
    return lax.dot_general(
        grad, weight, (((1,), (1,)), ((), ())), preferred_element_type=jnp.float32
    )


def matmul(left, right):
    return jnp.dot(left, right, preferred_element_type=jnp.float32)


def column_sum(values):
    return jnp.sum(values, axis=0, keepdims=True)


def row_mean(values):
    return jnp.mean(values, axis=-1, keepdims=True)


def normalise(values):
    centre = values - row_mean(values)
    scale = lax.rsqrt(row_mean(centre * centre) + EPSILON)
    return centre * scale, scale


def norm_back(grad, gain, unit, scale):
    scaled = grad * gain
    return scale * (scaled - row_mean(scaled) - unit * row_mean(scaled * unit))


class Chunks:
    def __init__(self, blocks, row, shape):
        self.blocks, self.row = blocks, row
        self.rows, self.columns = shape
        self.width = blocks.shape[2]

    def where(self, key):
        if key is Ellipsis:
            key = (slice(None), slice(0, self.width))
        height, span = key
        if self.columns > self.width:
            start = self.row + span.start // self.width * self.rows
            return slice(None), slice(start, start + self.rows)
        devices = slice(None)
        if height.start is not None:
            devices = slice(height.start // self.rows, height.stop // self.rows)
        return devices, slice(self.row, self.row + self.rows)

    def __setitem__(self, key, value):
        devices, rows = self.where(key)
        parts = value.reshape(-1, self.rows, self.width)
        self.blocks[devices, rows, :] = parts.astype(self.blocks.dtype)

    def __getitem__(self, key):
        devices, rows = self.where(key)
        parts = self.blocks[devices, rows, :]
        if self.rows % 16 != 0:
            parts = parts.astype(jnp.float32)
        return parts.reshape(-1, self.width).astype(self.blocks.dtype)


class Cast:
    def __init__(self, ref):
        self.ref = ref

    def __setitem__(self, key, value):
        self.ref[key] = value.astype(self.ref.dtype)


def dense_kernel(*refs):
    layer_kernel(*refs[:18], *[Cast(ref) for ref in refs[18:22]], *refs[22:])


def packed_kernel(shapes, *refs):
    blocks, terms = refs[4], refs[15]
    weights, grads, row = [], [], 0
    for shape in shapes:
        weights.append(Chunks(blocks, row, shape))
        grads.append(Chunks(terms, row, shape))
        row += shape[0] * (shape[1] // blocks.shape[2])
    width = blocks.shape[2]
    for index, dense in enumerate(refs[33:36]):
        for start in range(0, dense.shape[1], width):
            span = slice(start, start + width)
            dense[:, span] = weights[index][:, span]
        weights[index] = dense
    layer_kernel(*refs[:4], *weights, *refs[5:15], *grads, *refs[16:33])


def layer_kernel(
    hidden_ref,
    cotangent_ref,
    alive_ref,
    same_ref,
    w_qkv,
    w_out,
    w_in,
    w_back,
    bias_qkv,
    b_out,
    gain_one,
    shift_one,
    b_in,
    b_back,
    gain_two,
    shift_two,
    output_ref,
    grad_hidden_ref,
    dw_qkv,
    dw_out,
    dw_in,
    dw_back,
    db_qkv,
    db_out,
    dgain_one,
    dshift_one,
    db_in,
    db_back,
    dgain_two,
    dshift_two,
    qkv_ref,
    probs_ref,
    attended_ref,
    unit_one_ref,
    gated_ref,
    slope_ref,
    grad_sum_ref,
    grad_attended_ref,
    grad_qkv_ref,
):
    low, wide = jnp.bfloat16, jnp.float32
    rows, width = hidden_ref.shape
    factor = HEAD_DIM ** (-0.5)
    pair_width = 2 * HEAD_DIM
    alive = alive_ref[...]
    hidden_width = gated_ref.shape[1]
    spans = [slice(start, start + width) for start in range(0, hidden_width, width)]
    left_half = lax.broadcasted_iota(jnp.int32, (rows, pair_width), 1) < HEAD_DIM

    for part in range(3):
        span = slice(part * width, (part + 1) * width)
        projected = matmul(hidden_ref[...], w_qkv[:, span]) + bias_qkv[:, span]
        if part == 0:
            projected = projected * factor
        qkv_ref[:, span] = projected.astype(low)

    def pair_span(part, pair):
        start = part * width + pair * pair_width
        return slice(start, start + pair_width)

    def halves(values):
        zero = jnp.zeros_like(values)
        return jnp.where(left_half, values, zero), jnp.where(left_half, zero, values)

    pairs = width // pair_width
    for pair in range(pairs):
        queries = qkv_ref[:, pair_span(0, pair)]
        keys = qkv_ref[:, pair_span(1, pair)]
        values = qkv_ref[:, pair_span(2, pair)]
        found = []
        for half, part in enumerate(halves(queries)):
            scores = jnp.where(same_ref[...] > 0, back_product(part, keys), -1e30)
            expo = jnp.exp(scores - jnp.max(scores, axis=-1, keepdims=True))
            probs = expo * (1.0 / jnp.sum(expo, axis=-1, keepdims=True))
            probs_ref[2 * pair + half] = probs
            found.append(matmul(probs.astype(low), values))
        attended = jnp.where(left_half, found[0], found[1]) * alive
        attended_ref[:, pair_span(0, pair)] = attended.astype(low)

    summed_one = hidden_ref[...].astype(wide) + matmul(attended_ref[...], w_out[...]) + b_out[...]
    unit_one, scale_one = normalise(summed_one)
    unit_one_ref[...] = unit_one
    normed_one = unit_one * gain_one[...] + shift_one[...]
    normed_low = normed_one.astype(low)
    summed_two = normed_one + b_back[...]
    for span in spans:
        inner = matmul(normed_low, w_in[:, span]) + b_in[:, span]
        below = 0.5 + 0.5 * lax.erf(inner * 0.7071067811865476)
        slope_ref[:, span] = below + inner * (0.3989422804014327 * jnp.exp(-0.5 * inner * inner))
        gated = (inner * below).astype(low)
        gated_ref[:, span] = gated
        summed_two = summed_two + matmul(gated, w_back[span, :])
    unit_two, scale_two = normalise(summed_two)
    output_ref[...] = ((unit_two * gain_two[...] + shift_two[...]) * alive).astype(low)

    grad_out = cotangent_ref[...].astype(wide) * alive
    dgain_two[...] = column_sum(grad_out * unit_two)
    dshift_two[...] = column_sum(grad_out)
    grad_sum_two = norm_back(grad_out, gain_two[...], unit_two, scale_two)
    branch_two = grad_sum_two.astype(low)
    db_back[...] = column_sum(branch_two.astype(wide))
    grad_normed = grad_sum_two
    for span in spans:
        dw_back[span, :] = outer_sum(gated_ref[:, span], branch_two)
        grad_inner = (back_product(branch_two, w_back[span, :]) * slope_ref[:, span]).astype(low)
        db_in[:, span] = column_sum(grad_inner.astype(wide))
        dw_in[:, span] = outer_sum(normed_low, grad_inner)
        grad_normed = grad_normed + back_product(grad_inner, w_in[:, span])
    unit_one = unit_one_ref[...]
    dgain_one[...] = column_sum(grad_normed * unit_one)
    dshift_one[...] = column_sum(grad_normed)
    grad_sum_one = norm_back(grad_normed, gain_one[...], unit_one, scale_one)
    grad_sum_ref[...] = grad_sum_one
    branch_one = grad_sum_one.astype(low)
    db_out[...] = column_sum(branch_one.astype(wide))
    dw_out[...] = outer_sum(attended_ref[...], branch_one)
    grad_attended_ref[...] = (back_product(branch_one, w_out[...]) * alive).astype(low)

    for pair in range(pairs):
        queries = qkv_ref[:, pair_span(0, pair)]
        keys = qkv_ref[:, pair_span(1, pair)]
        values = qkv_ref[:, pair_span(2, pair)]
        grad_attended = grad_attended_ref[:, pair_span(0, pair)]
        found = []
        for half, part in enumerate(halves(grad_attended)):
            probs = probs_ref[2 * pair + half]
            grad_probs = back_product(part, values)
            inner_dot = jnp.sum(probs * grad_probs, axis=-1, keepdims=True)
            grad_scores = (probs * (grad_probs - inner_dot)).astype(low)
            found.append(
                (
                    matmul(grad_scores, keys) * factor,
                    outer_sum(grad_scores, queries),
                    outer_sum(probs.astype(low), grad_attended),
                )
            )
        for part in range(3):
            joined = jnp.where(left_half, found[0][part], found[1][part])
            grad_qkv_ref[:, pair_span(part, pair)] = joined.astype(low)

    grad_hidden = grad_sum_ref[...]
    for part in range(3):
        span = slice(part * width, (part + 1) * width)
        grad_part = grad_qkv_ref[:, span]
        db_qkv[:, span] = column_sum(grad_part.astype(wide))
        dw_qkv[:, span] = outer_sum(hidden_ref[...], grad_part)
        grad_hidden = grad_hidden + back_product(grad_part, w_qkv[:, span])
    grad_hidden_ref[...] = grad_hidden.astype(low)


def layer(hidden, cotangent, alive, same, weights, lines, shapes=None):
    rows, width = hidden.shape
    heads, hidden_width = width // HEAD_DIM, lines[4].shape[1]
    low, wide = jnp.bfloat16, jnp.float32
    shape = jax.ShapeDtypeStruct
    outs = (
        [shape(hidden.shape, low)] * 2
        + [shape(weight.shape, low) for weight in weights]
        + [shape(line.shape, wide) for line in lines]
    )
    scratch = [
        pltpu.VMEM((rows, 3 * width), low),
        pltpu.VMEM((heads, rows, rows), wide),
        pltpu.VMEM((rows, width), low),
        pltpu.VMEM((rows, width), wide),
        pltpu.VMEM((rows, hidden_width), low),
        pltpu.VMEM((rows, hidden_width), wide),
        pltpu.VMEM((rows, width), wide),
        pltpu.VMEM((rows, width), low),
        pltpu.VMEM((rows, 3 * width), low),
    ]
    kernel = dense_kernel
    if shapes is not None:
        kernel = functools.partial(packed_kernel, shapes)
        count = weights[0].shape[0]
        scratch += [pltpu.VMEM((count * part[0], part[1]), low) for part in shapes[:3]]
    return pl.pallas_call(
        kernel,
        out_shape=outs,
        in_specs=[pl.BlockSpec(memory_space=pltpu.VMEM)] * (4 + len(weights) + len(lines)),
        out_specs=[pl.BlockSpec(memory_space=pltpu.VMEM)] * len(outs),
        scratch_shapes=scratch,
        compiler_params=pltpu.CompilerParams(vmem_limit_bytes=VMEM_LIMIT),
    )(hidden, cotangent, alive, same, *weights, *lines)


def shards(
    hidden,
    cotangent,
    seq_lengths,
    w_qkv,
    b_qv,
    w_out,
    b_out,
    gain_one,
    shift_one,
    w_in,
    b_in,
    w_back,
    b_back,
    gain_two,
    shift_two,
):
    row_count, model_width = hidden.shape
    alive_row, same_seq = seq_masks(seq_lengths, row_count)
    alive_col = alive_row.astype(jnp.float32)[:, None]
    count = lax.axis_size("fsdp")
    weights = (w_qkv, w_out, w_in, w_back)
    biases = (b_qv, b_out, gain_one, shift_one, b_in, b_back, gain_two, shift_two)
    weight_shapes = [weight.shape for weight in weights]
    bias_sizes = [bias.shape[0] for bias in biases]
    block = pack(
        [weight[None] for weight in weights],
        [bias[None] for bias in biases],
        model_width,
        jnp.bfloat16,
    )[0]
    blocks = gather_blocks(block, count)
    full_weights, full_biases = unpack(blocks, weight_shapes, bias_sizes)
    used = sum(shape[0] * (shape[1] // model_width) for shape in weight_shapes)
    in_blocks = (
        all(shape[0] % 8 == 0 for shape in weight_shapes)
        and w_back.shape[0] % 16 == 0
        and used % 16 == 0
    )
    (
        full_bqv,
        full_bout,
        full_gone,
        full_sone,
        full_bin,
        full_bback,
        full_gtwo,
        full_stwo,
    ) = full_biases
    bias_qkv = jnp.concatenate(
        [
            full_bqv[:model_width],
            jnp.zeros((model_width,), full_bqv.dtype),
            full_bqv[model_width:],
        ]
    )
    lines = [
        line.astype(jnp.float32)[None]
        for line in (
            bias_qkv,
            full_bout,
            full_gone,
            full_sone,
            full_bin,
            full_bback,
            full_gtwo,
            full_stwo,
        )
    ]
    same = same_seq.astype(jnp.float32)
    if in_blocks:
        results = layer(hidden, cotangent, alive_col, same, (blocks,), lines, weight_shapes)
    else:
        results = layer(hidden, cotangent, alive_col, same, full_weights, lines)
    output, grad_hidden = results[:2]
    line_terms = [line[0] for line in results[-len(lines) :]]
    line_terms[0] = jnp.concatenate(
        [line_terms[0][:model_width], line_terms[0][2 * model_width :]]
    )
    line_terms = [line.reshape(count, -1) for line in line_terms]
    if in_blocks:
        tail = pack([], line_terms, model_width, jnp.bfloat16)
        terms = lax.dynamic_update_slice(results[2], tail, (0, used, 0))
    else:
        terms = pack(
            [term.reshape(count, -1, term.shape[1]) for term in results[2:6]],
            line_terms,
            model_width,
            jnp.bfloat16,
        )
    (share_qkv, share_out, share_in, share_back), vectors = unpack(
        scatter_blocks(terms)[None], weight_shapes, bias_sizes
    )
    return (
        output,
        grad_hidden,
        share_qkv,
        vectors[0],
        share_out,
        vectors[1],
        vectors[2],
        vectors[3],
        share_in,
        vectors[4],
        share_back,
        vectors[5],
        vectors[6],
        vectors[7],
    )


def solution(mesh):
    return jax.shard_map(
        shards,
        mesh=mesh,
        in_specs=(
            P("fsdp", None),
            P("fsdp", None),
            P("fsdp"),
            P("fsdp", None),
            P("fsdp"),
            P("fsdp", None),
            P("fsdp"),
            P("fsdp"),
            P("fsdp"),
            P("fsdp", None),
            P("fsdp"),
            P("fsdp", None),
            P("fsdp"),
            P("fsdp"),
            P("fsdp"),
        ),
        out_specs=(
            P("fsdp", None),
            P("fsdp", None),
            P("fsdp", None),
            P("fsdp"),
            P("fsdp", None),
            P("fsdp"),
            P("fsdp"),
            P("fsdp"),
            P("fsdp", None),
            P("fsdp"),
            P("fsdp", None),
            P("fsdp"),
            P("fsdp"),
            P("fsdp"),
        ),
        check_vma=False,
    )
```
